32 devices in a mesh: req: 8 (over z, y), tp: 4 (over x, core).
Axes of the slice: x: 2, y: 2, z: 4, core: 2. Of those that a mesh axis runs over, the one named last changes fastest.
Arguments:
- queries: bfloat16 [8, 1280, 24, 128], P('req', None, 'tp'), may hold values from -25 to 25
- text_kv: bfloat16 [8, 1280, 4, 256], P('req', None, 'tp'), may hold values from -6 to 6
- image_rows: bfloat16 [4096, 6144], P('req', 'tp'), may hold values from -6 to 6
- row_request: int32 [4096], P('req'), may hold values from 0 to 7, as said below
- row_position: int32 [4096], P('req'), may hold values from 8 to 1263, as said below
- prompt_lengths: int32 [8], P('req'), may hold values from 24 to 1280, as said below
- kv_weight: bfloat16 [6144, 4, 256], P('tp'), may hold values from -0.078125 to 0.078125
Outputs:
- attended: bfloat16 [8, 1280, 24, 128], P('req', None, 'tp')
The draws below stay inside these ranges and needn't reach their ends.
Inputs may be any that keep to these rules, and one draw needn't show every extreme that they name: `row_request`: the rows of one device name one request at most 128 times, and on every device some request is named exactly 128 times. `row_position`: the rows naming one request take distinct positions, 8 or more, that form one run ending at least 16 positions before that request's length. `prompt_lengths`: some request has length exactly 1280.
All inputs are finite; a program needn't handle non-finite values.
Results may differ from the reference program's by a relative error of at most 0.0085.
Values may be sent and summed in bfloat16 or wider, within the bound.
A program may use at most 128 MiB of HBM per device.

```python
import math
import jax
import jax.numpy as jnp
from jax import lax

D = 6144
HD = 128
QH = 24
KVH = 4
PROMPT = 1280
IMG_DEV = 512
REQS = 8
IMG_ROWS = 4096
CAP = 128


def layout(key):
    key_caps, key_first, key_noise, key_order, key_offset, key_tail = jax.random.split(jax.random.fold_in(key, 5), 6)
    total = REQS * CAP
    per_cap = jax.random.randint(key_caps, (REQS,), CAP // 2, CAP + 1)
    forced_req = jax.random.randint(key_first, (REQS,), 0, REQS)
    slot_req = jnp.arange(total, dtype=jnp.int32) // CAP
    slot_num = jnp.arange(total, dtype=jnp.int32) % CAP
    noise = jax.random.randint(key_noise, (REQS, total), 1, 2 ** 20 - 1)
    live = slot_num[None, :] < per_cap[slot_req][None, :]
    forced = slot_req[None, :] == forced_req[:, None]
    score = jnp.where(forced, 0, jnp.where(live, noise, 2 ** 20 - 1))
    score = score * total + jnp.arange(total, dtype=jnp.int32)[None, :]
    chosen = jnp.argsort(score, axis=1)[:, :IMG_DEV]
    dest = slot_req[chosen]
    shuffle_key = jax.random.randint(key_order, (REQS, IMG_DEV), 0, 2 ** 20) * IMG_DEV + jnp.arange(IMG_DEV, dtype=jnp.int32)[None, :]
    shuffle = jnp.argsort(shuffle_key, axis=1)
    dest = jnp.take_along_axis(dest, shuffle, axis=1).reshape(-1).astype(jnp.int32)
    one_hot = (dest[:, None] == jnp.arange(REQS, dtype=jnp.int32)[None, :]).astype(jnp.int32)
    rank = jnp.sum((jnp.cumsum(one_hot, axis=0) - one_hot) * one_hot, axis=1)
    counts = jnp.sum(one_hot, axis=0)
    request_ids = jnp.arange(REQS, dtype=jnp.int32)
    longest = jnp.argmax(counts).astype(jnp.int32)
    others = jnp.where(request_ids == longest, -1, counts)
    second = jnp.argmax(others).astype(jnp.int32)
    offset = jax.random.randint(key_offset, (REQS,), 8, 64)
    offset = jnp.where(request_ids == longest, PROMPT - 16 - counts, jnp.where(request_ids == second, 8, offset)).astype(jnp.int32)
    position = (offset[dest] + rank).astype(jnp.int32)
    room = PROMPT - offset - counts
    tail = jax.random.randint(key_tail, (REQS,), 16, room + 1)
    lengths = jnp.where(request_ids == longest, PROMPT, offset + counts + tail).astype(jnp.int32)
    return (dest, position, lengths)


def draw_row_request(key, part):
    return layout(key)[0]


def draw_row_position(key, part):
    return layout(key)[1]


def draw_prompt_lengths(key, part):
    return layout(key)[2]


def draw_queries(key, part):
    own_key = jax.random.fold_in(key, 21)
    base = jnp.clip(jax.random.normal(own_key, (REQS, PROMPT, QH, HD), jnp.float32), -6.0, 6.0)
    return base.astype(jnp.bfloat16)


def draw_text_kv(key, part):
    own_key = jax.random.fold_in(key, 31)
    base = jnp.clip(jax.random.normal(own_key, (REQS, PROMPT, KVH, 2 * HD), jnp.float32), -6.0, 6.0)
    return base.astype(jnp.bfloat16)


def block_scale(key, shape, cuts, smallest, largest):
    factor_of, own = 1.0, jax.random.fold_in(key, 6)
    for dim, parts in cuts:
        steps = jnp.exp(jax.random.uniform(jax.random.fold_in(own, dim), (parts,), jnp.float32, smallest / len(cuts), largest / len(cuts)))
        factor_of = factor_of * jnp.repeat(steps, shape[dim] // parts).reshape([-1 if axis == dim else 1 for axis in range(len(shape))])
    return factor_of


def bell_draw(key, shape, scale, limit, cuts=(), kind=jnp.bfloat16):
    values = scale * jax.random.normal(key, shape, jnp.float32)
    if cuts:
        values = values * block_scale(key, shape, cuts, -0.22, 0.18)
    return jnp.clip(values, -limit, limit).astype(kind)


def setup_inputs(seed: int = 0) -> dict:
    key_of = jax.random.split(jax.random.key(seed), 8)
    queries = draw_queries(jax.random.fold_in(key_of[7], 71), 0)
    text_kv = draw_text_kv(jax.random.fold_in(key_of[7], 71), 0)
    image_rows = bell_draw(key_of[2], (IMG_ROWS, D), 1.0, 6.0, ((0, 8), (1, 4)))
    row_request = draw_row_request(jax.random.fold_in(key_of[7], 71), 0)
    row_position = draw_row_position(jax.random.fold_in(key_of[7], 71), 0)
    prompt_lengths = draw_prompt_lengths(jax.random.fold_in(key_of[7], 71), 0)
    kv_weight = bell_draw(key_of[6], (D, KVH, 2 * HD), D ** -0.5, 0.078125, ((0, 4),))
    return {"queries": queries, "text_kv": text_kv, "image_rows": image_rows, "row_request": row_request, "row_position": row_position, "prompt_lengths": prompt_lengths, "kv_weight": kv_weight}


def rotate_keys(summed, positions, head_dim):
    half = head_dim // 2
    freqs = jnp.exp(jnp.arange(half, dtype=jnp.float32) * (-2.0 * math.log(1000000.0) / head_dim))
    angles = positions.astype(jnp.float32)[:, None, None] * freqs[None, None, :]
    cosine = jnp.cos(angles)
    sine = jnp.sin(angles)
    first = summed[..., :half]
    second = summed[..., half:head_dim]
    rotated = jnp.concatenate([first * cosine - second * sine, second * cosine + first * sine, summed[..., head_dim:]], axis=-1)
    return rotated.astype(jnp.bfloat16)


def attend(args):
    query_rows, prompt_kv, length = args
    group = QH // KVH
    grouped = query_rows.reshape(PROMPT, KVH, group, HD).astype(jnp.float32)
    keys = prompt_kv[..., :HD].astype(jnp.float32)
    values = prompt_kv[..., HD:].astype(jnp.float32)
    scores = jnp.einsum("qhgd,khd->hgqk", grouped, keys) * (HD ** -0.5)
    index = jnp.arange(PROMPT, dtype=jnp.int32)
    allowed = (index[None, :] <= index[:, None]) & (index[None, :] < length)
    scores = jnp.where(allowed, scores, jnp.float32(-1e30))
    highest = jnp.max(scores, axis=-1, keepdims=True)
    expo = jnp.exp(scores - highest)
    weights = (expo / jnp.sum(expo, axis=-1, keepdims=True)).astype(jnp.bfloat16)
    result = jnp.einsum("hgqk,khd->qhgd", weights.astype(jnp.float32), values)
    result = jnp.where(index[:, None, None, None] < length, result, jnp.float32(0.0))
    return result.reshape(PROMPT, QH, HD).astype(jnp.bfloat16)


def reference(queries, text_kv, image_rows, row_request, row_position, prompt_lengths, kv_weight):
    summed = jnp.dot(image_rows, kv_weight.reshape(D, KVH * 2 * HD), preferred_element_type=jnp.float32)
    summed = summed.reshape(IMG_ROWS, KVH, 2 * HD)
    image_kv = rotate_keys(summed, row_position, HD)
    prompt_kv = text_kv.at[row_request, row_position].set(image_kv)
    return lax.map(attend, (queries, prompt_kv, prompt_lengths))
```

```python
import functools
import math

import jax
import jax.numpy as jnp
import numpy as np
from jax import lax
from jax.experimental import pallas as pl
from jax.experimental.pallas import tpu as pltpu
from jax.sharding import PartitionSpec as P

MESH = pl.DeviceIdType.MESH
NT = (((1,), (1,)), ((), ()))
VMEM = pltpu.VMEM
Q_BLOCK = 256


def route_kernel(
    groups,
    capacity,
    partial_ref,
    request_ref,
    position_ref,
    freq_ref,
    kv_ref,
    place_ref,
    from_core,
    to_chip,
    from_chip,
    hot_ref,
    bins_ref,
    place_bins,
    core_send,
    core_recv,
    chip_send,
    chip_recv,
    kv_send,
    kv_recv,
    place_send,
    place_recv,
):
    me = lax.axis_index("req")
    tp = lax.axis_index("tp")
    side = lax.rem(tp, 2)
    half = tp // 2
    mate = half * 2 + (1 - side)
    far = (1 - half) * 2 + side
    rows = partial_ref.shape[1]
    width = kv_ref.shape[2]

    barrier = pltpu.get_barrier_semaphore()

    def greet(step, carry):
        pl.semaphore_signal(
            barrier, inc=1, device_id={"req": lax.rem(me + step, groups)}, device_id_type=MESH
        )
        return carry

    lax.fori_loop(1, groups, greet, 0)
    for partner in (mate, far):
        pl.semaphore_signal(barrier, inc=1, device_id={"tp": partner}, device_id_type=MESH)

    request = request_ref[...]
    hot = (request == lax.broadcasted_iota(jnp.int32, (groups, rows), 0)).astype(jnp.float32)
    row_id = lax.broadcasted_iota(jnp.int32, (rows, rows), 0)
    column_id = lax.broadcasted_iota(jnp.int32, (rows, rows), 1)
    earlier = (row_id < column_id).astype(jnp.float32).astype(jnp.bfloat16)
    before = jnp.dot(hot.astype(jnp.bfloat16), earlier, preferred_element_type=jnp.float32)
    rank = jnp.sum(before * hot, axis=0, keepdims=True)
    target = request.astype(jnp.float32) * float(capacity) + rank
    position = position_ref[...]

    pl.semaphore_wait(barrier, groups + 1)

    def core_copy(part):
        columns = pl.ds(part * width, width)
        copies = []
        for index in range(2):
            copies.append(
                pltpu.make_async_remote_copy(
                    src_ref=partial_ref.at[index * 2 + 1 - side, :, columns],
                    dst_ref=from_core.at[part, index],
                    send_sem=core_send.at[part, index],
                    recv_sem=core_recv.at[part, index],
                    device_id={"tp": mate},
                    device_id_type=MESH,
                )
            )
        return copies

    core_copies = [core_copy(part) for part in range(2)]
    for part in range(2):
        for index in range(2):
            core_copies[part][index].start()

    slots = groups * capacity
    hot_ref[...] = (
        (target == lax.broadcasted_iota(jnp.int32, (slots, rows), 0).astype(jnp.float32))
        .astype(jnp.float32)
        .astype(jnp.bfloat16)
    )
    coded = position + 1
    line = lax.broadcasted_iota(jnp.int32, (16, rows), 0)
    digits = (
        jnp.where(line < 8, coded // 32, lax.rem(coded, 32)).astype(jnp.float32).astype(jnp.bfloat16)
    )

    def place_copy(dest):
        return pltpu.make_async_remote_copy(
            src_ref=place_bins.at[dest],
            dst_ref=place_ref.at[me],
            send_sem=place_send.at[dest],
            recv_sem=place_recv.at[me],
            device_id={"req": dest},
            device_id_type=MESH,
        )

    def bin_places(dest):
        found = lax.dot_general(
            digits,
            hot_ref[pl.ds(pl.multiple_of(dest * capacity, capacity), capacity), :],
            NT,
            preferred_element_type=jnp.float32,
        )
        return (found[:8] * 32.0 + found[8:]).astype(jnp.int32)

    def send_places(step, carry):
        dest = lax.rem(me + step, groups)
        place_bins[dest] = bin_places(dest)
        place_copy(dest).start()
        return carry

    lax.fori_loop(1, groups, send_places, 0)
    place_ref[me] = bin_places(me)

    chip_copies = []
    for part in range(2):
        columns = pl.ds(part * width, width)
        for index in range(2):
            core_copies[part][index].wait()
        other = 1 - half
        to_chip[part] = (
            partial_ref[other * 2 + side, :, columns] + from_core[part, other]
        ).astype(jnp.bfloat16)
        copy = pltpu.make_async_remote_copy(
            src_ref=to_chip.at[part],
            dst_ref=from_chip.at[part],
            send_sem=chip_send.at[part],
            recv_sem=chip_recv.at[part],
            device_id={"tp": far},
            device_id_type=MESH,
        )
        copy.start()
        chip_copies.append(copy)

    place_column = jnp.sum(
        jnp.where(row_id == column_id, position.astype(jnp.float32), 0.0), axis=1, keepdims=True
    )
    angle = place_column * freq_ref[...]
    cosine = jnp.cos(angle)
    lane = lax.broadcasted_iota(jnp.int32, (rows, width), 1)
    sine = jnp.where(lane < width // 2, -1.0, 1.0) * jnp.sin(angle)

    def kv_copy(part, dest):
        return pltpu.make_async_remote_copy(
            src_ref=bins_ref.at[part, dest],
            dst_ref=kv_ref.at[part, pl.ds(pl.multiple_of(me * capacity, capacity), capacity)],
            send_sem=kv_send.at[part, dest],
            recv_sem=kv_recv.at[part, me],
            device_id={"req": dest},
            device_id_type=MESH,
        )

    for part in range(2):
        columns = pl.ds(part * width, width)
        chip_copies[part].wait()
        summed = (
            partial_ref[half * 2 + side, :, columns]
            + from_core[part, half]
            + from_chip[part].astype(jnp.float32)
        )
        if part == 0:
            summed = summed * cosine + pltpu.roll(summed, width // 2, 1) * sine
        image = summed.astype(jnp.bfloat16)

        def bin_rows(dest, image=image):
            return jnp.dot(
                hot_ref[pl.ds(pl.multiple_of(dest * capacity, capacity), capacity), :],
                image,
                preferred_element_type=jnp.float32,
            ).astype(jnp.bfloat16)

        def send_rows(step, carry, part=part, bin_rows=bin_rows):
            dest = lax.rem(me + step, groups)
            bins_ref[part, dest] = bin_rows(dest)
            kv_copy(part, dest).start()
            return carry

        lax.fori_loop(1, groups, send_rows, 0)
        kv_ref[part, pl.ds(pl.multiple_of(me * capacity, capacity), capacity)] = bin_rows(me)

    def finish(step, carry):
        peer = lax.rem(me + step, groups)
        place_copy(peer).wait_send()
        pltpu.make_async_copy(
            place_bins.at[peer], place_ref.at[peer], place_recv.at[peer]
        ).wait()
        for part in range(2):
            kv_copy(part, peer).wait_send()
            pltpu.make_async_copy(
                bins_ref.at[part, peer],
                kv_ref.at[part, pl.ds(pl.multiple_of(peer * capacity, capacity), capacity)],
                kv_recv.at[part, peer],
            ).wait()
        return carry

    lax.fori_loop(1, groups, finish, 0)


def route(partial, row_request, row_position, groups, capacity):
    heads, rows, both = partial.shape
    width = both // 2
    slots = groups * capacity
    exponent = np.arange(width // 2, dtype=np.float32) * np.float32(
        -2.0 * math.log(1000000.0) / width
    )
    freqs = np.exp(exponent.astype(np.float32)).astype(np.float32)
    freqs = jnp.asarray(np.concatenate([freqs, freqs])[None])
    vmem = pl.BlockSpec(memory_space=VMEM)
    return pl.pallas_call(
        functools.partial(route_kernel, groups, capacity),
        out_shape=(
            jax.ShapeDtypeStruct((2, slots, width), jnp.bfloat16),
            jax.ShapeDtypeStruct((groups, 8, capacity), jnp.int32),
        ),
        in_specs=[vmem] * 4,
        out_specs=(vmem, vmem),
        scratch_shapes=[
            VMEM((2, 2, rows, width), jnp.float32),
            VMEM((2, rows, width), jnp.bfloat16),
            VMEM((2, rows, width), jnp.bfloat16),
            VMEM((slots, rows), jnp.bfloat16),
            VMEM((2, groups, capacity, width), jnp.bfloat16),
            VMEM((groups, 8, capacity), jnp.int32),
            pltpu.SemaphoreType.DMA((2, 2)),
            pltpu.SemaphoreType.DMA((2, 2)),
            pltpu.SemaphoreType.DMA((2,)),
            pltpu.SemaphoreType.DMA((2,)),
            pltpu.SemaphoreType.DMA((2, groups)),
            pltpu.SemaphoreType.DMA((2, groups)),
            pltpu.SemaphoreType.DMA((groups,)),
            pltpu.SemaphoreType.DMA((groups,)),
        ],
        compiler_params=pltpu.CompilerParams(
            collective_id=0, has_side_effects=True, vmem_limit_bytes=32 * 1024 * 1024
        ),
        name="route",
    )(partial, row_request[None], row_position[None], freqs)


def attend_kernel(length_ref, query_ref, text_ref, kv_ref, place_ref, out_ref, keys, values):
    prompt, width = keys.shape
    slots = kv_ref.shape[1]

    @pl.when(pl.program_id(0) == 0)
    def _():
        if place_ref.shape[0] > 1:
            places = jnp.concatenate(
                [place_ref[source, 0:1, :] for source in range(place_ref.shape[0])], axis=1
            )
        else:
            places = place_ref[0, 0:1, :]
        places = places - 1
        first = jnp.min(jnp.where(places < 0, prompt, places), axis=1, keepdims=True)
        last = jnp.max(places, axis=1, keepdims=True)
        for start in range(0, prompt, Q_BLOCK):
            block = pl.ds(start, Q_BLOCK)
            index = lax.broadcasted_iota(jnp.int32, (Q_BLOCK, slots), 0) + start
            hot = (index == places).astype(jnp.float32).astype(jnp.bfloat16)
            own = lax.broadcasted_iota(jnp.int32, (Q_BLOCK, width), 0) + start
            image = (own >= first) & (own <= last)
            for part, held in ((0, keys), (1, values)):
                found = jnp.dot(hot, kv_ref[part], preferred_element_type=jnp.float32)
                text = text_ref[block, part * width : (part + 1) * width].astype(jnp.float32)
                held[block, 0:width] = jnp.where(image, found, text).astype(jnp.bfloat16)
        values[:, width:] = jnp.ones((prompt, width), jnp.bfloat16)

    length = length_ref[0]
    factor = width**-0.5 * math.log2(math.e)
    for start in range(0, prompt, Q_BLOCK):
        stop = start + Q_BLOCK
        query = query_ref[0, start:stop, :]
        scores = lax.dot_general(query, keys[:stop], NT, preferred_element_type=jnp.float32)
        row = lax.broadcasted_iota(jnp.int32, (Q_BLOCK, Q_BLOCK), 0)
        column = lax.broadcasted_iota(jnp.int32, (Q_BLOCK, Q_BLOCK), 1)
        diagonal = jnp.where(column <= row, scores[:, start:], jnp.float32(-1e30))
        if start:
            scores = jnp.concatenate([scores[:, :start], diagonal], axis=1)
        else:
            scores = diagonal
        highest = jnp.max(scores, axis=1, keepdims=True)
        expo = jnp.exp2((scores - highest) * factor).astype(jnp.bfloat16)
        result = jnp.dot(expo, values[:stop], preferred_element_type=jnp.float32)
        own = lax.broadcasted_iota(jnp.int32, (Q_BLOCK, width), 0) + start
        attended = jnp.where(own < length, result[:, :width] / result[:, width:], 0.0)
        out_ref[0, start:stop, :] = attended.astype(jnp.bfloat16)


def attend(queries, text, kv, places, lengths):
    heads, prompt, width = queries.shape
    return pl.pallas_call(
        attend_kernel,
        out_shape=jax.ShapeDtypeStruct(queries.shape, jnp.bfloat16),
        grid_spec=pltpu.PrefetchScalarGridSpec(
            num_scalar_prefetch=1,
            grid=(heads,),
            in_specs=[
                pl.BlockSpec((1, prompt, width), lambda head, _: (head, 0, 0)),
                pl.BlockSpec(text.shape, lambda head, _: (0, 0)),
                pl.BlockSpec(kv.shape, lambda head, _: (0, 0, 0)),
                pl.BlockSpec(places.shape, lambda head, _: (0, 0, 0)),
            ],
            out_specs=pl.BlockSpec((1, prompt, width), lambda head, _: (head, 0, 0)),
            scratch_shapes=[
                VMEM((prompt, width), jnp.bfloat16),
                VMEM((prompt, 2 * width), jnp.bfloat16),
            ],
        ),
        compiler_params=pltpu.CompilerParams(vmem_limit_bytes=48 * 1024 * 1024),
        name="attend",
    )(lengths, queries, text, kv, places)


def per_device(queries, text_kv, image_rows, row_request, row_position, prompt_lengths, kv_weight):
    groups = lax.axis_size("req")
    capacity = 2 * image_rows.shape[0] // groups
    partial = jnp.einsum(
        "rd,dhc->hrc", image_rows, kv_weight, preferred_element_type=jnp.float32
    )
    kv, places = route(partial, row_request, row_position, groups, capacity)
    if capacity % 128:
        places = jnp.broadcast_to(places[:, 0, :].reshape(1, 1, -1), (1, 8, groups * capacity))
    attended = attend(
        jnp.transpose(queries[0], (1, 0, 2)), text_kv[0, :, 0, :], kv, places, prompt_lengths
    )
    return jnp.transpose(attended, (1, 0, 2))[None]


def solution(mesh):
    in_specs = (
        P("req", None, "tp", None),
        P("req", None, "tp", None),
        P("req", "tp"),
        P("req"),
        P("req"),
        P("req"),
        P("tp", None, None),
    )
    out_specs = P("req", None, "tp", None)
    return jax.shard_map(
        per_device, mesh=mesh, in_specs=in_specs, out_specs=out_specs, check_vma=False
    )
```

```python
import functools
import math

import jax
import jax.numpy as jnp
import numpy as np
from jax import lax
from jax.experimental import pallas as pl
from jax.experimental.pallas import tpu as pltpu
from jax.sharding import PartitionSpec as P

MESH = pl.DeviceIdType.MESH
NT = (((1,), (1,)), ((), ()))
VMEM = pltpu.VMEM
Q_BLOCK = 256
HEAD_BLOCK = 3


def route_kernel(
    groups,
    capacity,
    partial_ref,
    request_ref,
    position_ref,
    freq_ref,
    kv_ref,
    place_ref,
    to_core,
    from_core,
    to_chip,
    from_chip,
    hot_ref,
    bins_ref,
    place_bins,
    core_send,
    core_recv,
    chip_send,
    chip_recv,
    kv_send,
    kv_recv,
    place_send,
    place_recv,
):
    me = lax.axis_index("req")
    tp = lax.axis_index("tp")
    side = lax.rem(tp, 2)
    half = tp // 2
    mate = half * 2 + (1 - side)
    far = (1 - half) * 2 + side
    rows = partial_ref.shape[1]
    width = kv_ref.shape[2]

    barrier = pltpu.get_barrier_semaphore()

    def greet(step, carry):
        pl.semaphore_signal(
            barrier, inc=1, device_id={"req": lax.rem(me + step, groups)}, device_id_type=MESH
        )
        return carry

    lax.fori_loop(1, groups, greet, 0)
    for partner in (mate, far):
        pl.semaphore_signal(barrier, inc=1, device_id={"tp": partner}, device_id_type=MESH)

    request = request_ref[...]
    hot = (request == lax.broadcasted_iota(jnp.int32, (groups, rows), 0)).astype(jnp.float32)
    row_id = lax.broadcasted_iota(jnp.int32, (rows, rows), 0)
    column_id = lax.broadcasted_iota(jnp.int32, (rows, rows), 1)
    earlier = (row_id < column_id).astype(jnp.float32).astype(jnp.bfloat16)
    before = jnp.dot(hot.astype(jnp.bfloat16), earlier, preferred_element_type=jnp.float32)
    rank = jnp.sum(before * hot, axis=0, keepdims=True)
    target = request.astype(jnp.float32) * float(capacity) + rank
    position = position_ref[...]
    for index in range(2):
        to_core[index] = partial_ref[index * 2 + 1 - side].astype(jnp.bfloat16)

    pl.semaphore_wait(barrier, groups + 1)

    def core_copy(part):
        columns = pl.ds(part * width, width)
        copies = []
        for index in range(2):
            copies.append(
                pltpu.make_async_remote_copy(
                    src_ref=to_core.at[index, :, columns],
                    dst_ref=from_core.at[part, index],
                    send_sem=core_send.at[part, index],
                    recv_sem=core_recv.at[part, index],
                    device_id={"tp": mate},
                    device_id_type=MESH,
                )
            )
        return copies

    core_copies = [core_copy(part) for part in range(2)]
    for part in range(2):
        for index in range(2):
            core_copies[part][index].start()

    slots = groups * capacity
    hot_ref[...] = (
        (target == lax.broadcasted_iota(jnp.int32, (slots, rows), 0).astype(jnp.float32))
        .astype(jnp.float32)
        .astype(jnp.bfloat16)
    )
    coded = position + 1
    line = lax.broadcasted_iota(jnp.int32, (16, rows), 0)
    digits = (
        jnp.where(line < 8, coded // 32, lax.rem(coded, 32)).astype(jnp.float32).astype(jnp.bfloat16)
    )

    def place_copy(dest):
        return pltpu.make_async_remote_copy(
            src_ref=place_bins.at[dest],
            dst_ref=place_ref.at[me],
            send_sem=place_send.at[dest],
            recv_sem=place_recv.at[me],
            device_id={"req": dest},
            device_id_type=MESH,
        )

    def bin_places(dest):
        found = lax.dot_general(
            digits,
            hot_ref[pl.ds(pl.multiple_of(dest * capacity, capacity), capacity), :],
            NT,
            preferred_element_type=jnp.float32,
        )
        return (found[:8] * 32.0 + found[8:]).astype(jnp.int32)

    def send_places(step, carry):
        dest = lax.rem(me + step, groups)
        place_bins[dest] = bin_places(dest)
        place_copy(dest).start()
        return carry

    lax.fori_loop(1, groups, send_places, 0)
    place_ref[me] = bin_places(me)

    chip_copies = []
    for part in range(2):
        columns = pl.ds(part * width, width)
        for index in range(2):
            core_copies[part][index].wait()
        other = 1 - half
        to_chip[part] = (
            partial_ref[other * 2 + side, :, columns] + from_core[part, other].astype(jnp.float32)
        ).astype(jnp.bfloat16)
        copy = pltpu.make_async_remote_copy(
            src_ref=to_chip.at[part],
            dst_ref=from_chip.at[part],
            send_sem=chip_send.at[part],
            recv_sem=chip_recv.at[part],
            device_id={"tp": far},
            device_id_type=MESH,
        )
        copy.start()
        chip_copies.append(copy)

    place_column = jnp.sum(
        jnp.where(row_id == column_id, position.astype(jnp.float32), 0.0), axis=1, keepdims=True
    )
    angle = place_column * freq_ref[...]
    cosine = jnp.cos(angle)
    lane = lax.broadcasted_iota(jnp.int32, (rows, width), 1)
    sine = jnp.where(lane < width // 2, -1.0, 1.0) * jnp.sin(angle)

    def kv_copy(part, dest):
        return pltpu.make_async_remote_copy(
            src_ref=bins_ref.at[part, dest],
            dst_ref=kv_ref.at[part, pl.ds(pl.multiple_of(me * capacity, capacity), capacity)],
            send_sem=kv_send.at[part, dest],
            recv_sem=kv_recv.at[part, me],
            device_id={"req": dest},
            device_id_type=MESH,
        )

    for part in range(2):
        columns = pl.ds(part * width, width)
        chip_copies[part].wait()
        summed = (
            partial_ref[half * 2 + side, :, columns]
            + from_core[part, half].astype(jnp.float32)
            + from_chip[part].astype(jnp.float32)
        )
        if part == 0:
            summed = summed * cosine + pltpu.roll(summed, width // 2, 1) * sine
        image = summed.astype(jnp.bfloat16)

        def bin_rows(dest, image=image):
            return jnp.dot(
                hot_ref[pl.ds(pl.multiple_of(dest * capacity, capacity), capacity), :],
                image,
                preferred_element_type=jnp.float32,
            ).astype(jnp.bfloat16)

        def send_rows(step, carry, part=part, bin_rows=bin_rows):
            dest = lax.rem(me + step, groups)
            bins_ref[part, dest] = bin_rows(dest)
            kv_copy(part, dest).start()
            return carry

        lax.fori_loop(1, groups, send_rows, 0)
        kv_ref[part, pl.ds(pl.multiple_of(me * capacity, capacity), capacity)] = bin_rows(me)

    def finish(step, carry):
        peer = lax.rem(me + step, groups)
        place_copy(peer).wait_send()
        pltpu.make_async_copy(
            place_bins.at[peer], place_ref.at[peer], place_recv.at[peer]
        ).wait()
        for part in range(2):
            kv_copy(part, peer).wait_send()
            pltpu.make_async_copy(
                bins_ref.at[part, peer],
                kv_ref.at[part, pl.ds(pl.multiple_of(peer * capacity, capacity), capacity)],
                kv_recv.at[part, peer],
            ).wait()
        return carry

    lax.fori_loop(1, groups, finish, 0)


def route(partial, row_request, row_position, groups, capacity):
    heads, rows, both = partial.shape
    width = both // 2
    slots = groups * capacity
    exponent = np.arange(width // 2, dtype=np.float32) * np.float32(
        -2.0 * math.log(1000000.0) / width
    )
    freqs = np.exp(exponent.astype(np.float32)).astype(np.float32)
    freqs = jnp.asarray(np.concatenate([freqs, freqs])[None])
    vmem = pl.BlockSpec(memory_space=VMEM)
    return pl.pallas_call(
        functools.partial(route_kernel, groups, capacity),
        out_shape=(
            jax.ShapeDtypeStruct((2, slots, width), jnp.bfloat16),
            jax.ShapeDtypeStruct((groups, 8, capacity), jnp.int32),
        ),
        in_specs=[vmem] * 4,
        out_specs=(vmem, vmem),
        scratch_shapes=[
            VMEM((2, rows, both), jnp.bfloat16),
            VMEM((2, 2, rows, width), jnp.bfloat16),
            VMEM((2, rows, width), jnp.bfloat16),
            VMEM((2, rows, width), jnp.bfloat16),
            VMEM((slots, rows), jnp.bfloat16),
            VMEM((2, groups, capacity, width), jnp.bfloat16),
            VMEM((groups, 8, capacity), jnp.int32),
            pltpu.SemaphoreType.DMA((2, 2)),
            pltpu.SemaphoreType.DMA((2, 2)),
            pltpu.SemaphoreType.DMA((2,)),
            pltpu.SemaphoreType.DMA((2,)),
            pltpu.SemaphoreType.DMA((2, groups)),
            pltpu.SemaphoreType.DMA((2, groups)),
            pltpu.SemaphoreType.DMA((groups,)),
            pltpu.SemaphoreType.DMA((groups,)),
        ],
        compiler_params=pltpu.CompilerParams(
            collective_id=0, has_side_effects=True, vmem_limit_bytes=32 * 1024 * 1024
        ),
        name="route",
    )(partial, row_request[None], row_position[None], freqs)


def attend_kernel(length_ref, query_ref, text_ref, kv_ref, place_ref, out_ref, keys, values):
    prompt, width = keys.shape
    slots = kv_ref.shape[1]

    @pl.when(pl.program_id(0) == 0)
    def _():
        if place_ref.shape[0] > 1:
            places = jnp.concatenate(
                [place_ref[source, 0:1, :] for source in range(place_ref.shape[0])], axis=1
            )
        else:
            places = place_ref[0, 0:1, :]
        places = places - 1
        first = jnp.min(jnp.where(places < 0, prompt, places), axis=1, keepdims=True)
        last = jnp.max(places, axis=1, keepdims=True)
        for start in range(0, prompt, Q_BLOCK):
            block = pl.ds(start, Q_BLOCK)
            index = lax.broadcasted_iota(jnp.int32, (Q_BLOCK, slots), 0) + start
            hot = (index == places).astype(jnp.float32).astype(jnp.bfloat16)
            own = lax.broadcasted_iota(jnp.int32, (Q_BLOCK, width), 0) + start
            image = (own >= first) & (own <= last)
            for part, held in ((0, keys), (1, values)):
                found = jnp.dot(hot, kv_ref[part], preferred_element_type=jnp.float32)
                text = text_ref[block, part * width : (part + 1) * width].astype(jnp.float32)
                held[block, 0:width] = jnp.where(image, found, text).astype(jnp.bfloat16)
        values[:, width:] = jnp.ones((prompt, width), jnp.bfloat16)

    length = length_ref[0]
    factor = width**-0.5 * math.log2(math.e)
    row = lax.broadcasted_iota(jnp.int32, (Q_BLOCK, Q_BLOCK), 0)
    column = lax.broadcasted_iota(jnp.int32, (Q_BLOCK, Q_BLOCK), 1)

    def score(head, start):
        query = query_ref[head, start : start + Q_BLOCK, :]
        blocks = []
        for first in range(0, start + Q_BLOCK, Q_BLOCK):
            block = lax.dot_general(
                query, keys[first : first + Q_BLOCK], NT, preferred_element_type=jnp.float32
            )
            if first == start:
                block = jnp.where(column <= row, block, jnp.float32(-1e30))
            blocks.append(block)
        return blocks

    def weigh(head, start, blocks):
        highest = jnp.max(functools.reduce(jnp.maximum, blocks), axis=1, keepdims=True)
        result = None
        for index, block in enumerate(blocks):
            expo = jnp.exp2((block - highest) * factor).astype(jnp.bfloat16)
            part = jnp.dot(
                expo,
                values[index * Q_BLOCK : (index + 1) * Q_BLOCK],
                preferred_element_type=jnp.float32,
            )
            result = part if result is None else result + part
        own = lax.broadcasted_iota(jnp.int32, (Q_BLOCK, width), 0) + start
        attended = jnp.where(own < length, result[:, :width] / result[:, width:], 0.0)
        out_ref[head, start : start + Q_BLOCK, :] = attended.astype(jnp.bfloat16)

    steps = [
        (head, start) for head in range(query_ref.shape[0]) for start in range(0, prompt, Q_BLOCK)
    ]
    held = score(*steps[0])
    for index, step in enumerate(steps):
        later = score(*steps[index + 1]) if index + 1 < len(steps) else None
        weigh(*step, held)
        held = later


def attend(queries, text, kv, places, lengths):
    heads, prompt, width = queries.shape
    return pl.pallas_call(
        attend_kernel,
        out_shape=jax.ShapeDtypeStruct(queries.shape, jnp.bfloat16),
        grid_spec=pltpu.PrefetchScalarGridSpec(
            num_scalar_prefetch=1,
            grid=(heads // HEAD_BLOCK,),
            in_specs=[
                pl.BlockSpec((HEAD_BLOCK, prompt, width), lambda head, _: (head, 0, 0)),
                pl.BlockSpec(text.shape, lambda head, _: (0, 0)),
                pl.BlockSpec(kv.shape, lambda head, _: (0, 0, 0)),
                pl.BlockSpec(places.shape, lambda head, _: (0, 0, 0)),
            ],
            out_specs=pl.BlockSpec((HEAD_BLOCK, prompt, width), lambda head, _: (head, 0, 0)),
            scratch_shapes=[
                VMEM((prompt, width), jnp.bfloat16),
                VMEM((prompt, 2 * width), jnp.bfloat16),
            ],
        ),
        compiler_params=pltpu.CompilerParams(vmem_limit_bytes=48 * 1024 * 1024),
        name="attend",
    )(lengths, queries, text, kv, places)


def per_device(queries, text_kv, image_rows, row_request, row_position, prompt_lengths, kv_weight):
    groups = lax.axis_size("req")
    capacity = 2 * image_rows.shape[0] // groups
    partial = jnp.einsum(
        "rd,dhc->hrc", image_rows, kv_weight, preferred_element_type=jnp.float32
    )
    kv, places = route(partial, row_request, row_position, groups, capacity)
    if capacity % 128:
        places = jnp.broadcast_to(places[:, 0, :].reshape(1, 1, -1), (1, 8, groups * capacity))
    attended = attend(
        jnp.transpose(queries[0], (1, 0, 2)), text_kv[0, :, 0, :], kv, places, prompt_lengths
    )
    return jnp.transpose(attended, (1, 0, 2))[None]


def solution(mesh):
    in_specs = (
        P("req", None, "tp", None),
        P("req", None, "tp", None),
        P("req", "tp"),
        P("req"),
        P("req"),
        P("req"),
        P("tp", None, None),
    )
    out_specs = P("req", None, "tp", None)
    return jax.shard_map(
        per_device, mesh=mesh, in_specs=in_specs, out_specs=out_specs, check_vma=False
    )
```

```python
import functools
import math

import jax
import jax.numpy as jnp
import numpy as np
from jax import lax
from jax.experimental import pallas as pl
from jax.experimental.pallas import tpu as pltpu
from jax.sharding import PartitionSpec as P

MESH = pl.DeviceIdType.MESH
NT = (((1,), (1,)), ((), ()))
VMEM = pltpu.VMEM
Q_BLOCK = 256
HEAD_BLOCK = 3


def route_kernel(
    groups,
    capacity,
    partial_ref,
    request_ref,
    position_ref,
    freq_ref,
    kv_ref,
    place_ref,
    to_core,
    from_core,
    to_chip,
    from_chip,
    hot_ref,
    bins_ref,
    place_bins,
    core_send,
    core_recv,
    chip_send,
    chip_recv,
    kv_send,
    kv_recv,
    place_send,
    place_recv,
):
    me = lax.axis_index("req")
    tp = lax.axis_index("tp")
    side = lax.rem(tp, 2)
    half = tp // 2
    mate = half * 2 + (1 - side)
    far = (1 - half) * 2 + side
    rows = partial_ref.shape[1]
    width = kv_ref.shape[2]

    barrier = pltpu.get_barrier_semaphore()

    def greet(step, carry):
        pl.semaphore_signal(
            barrier, inc=1, device_id={"req": lax.rem(me + step, groups)}, device_id_type=MESH
        )
        return carry

    lax.fori_loop(1, groups, greet, 0)
    for partner in (mate, far):
        pl.semaphore_signal(barrier, inc=1, device_id={"tp": partner}, device_id_type=MESH)

    request = request_ref[...]
    hot = (request == lax.broadcasted_iota(jnp.int32, (groups, rows), 0)).astype(jnp.float32)
    row_id = lax.broadcasted_iota(jnp.int32, (rows, rows), 0)
    column_id = lax.broadcasted_iota(jnp.int32, (rows, rows), 1)
    earlier = (row_id < column_id).astype(jnp.float32).astype(jnp.bfloat16)
    before = jnp.dot(hot.astype(jnp.bfloat16), earlier, preferred_element_type=jnp.float32)
    rank = jnp.sum(before * hot, axis=0, keepdims=True)
    target = request.astype(jnp.float32) * float(capacity) + rank
    position = position_ref[...]
    for index in range(2):
        to_core[index] = partial_ref[index * 2 + 1 - side].astype(jnp.bfloat16)

    pl.semaphore_wait(barrier, groups + 1)

    def core_copy(part):
        columns = pl.ds(part * width, width)
        copies = []
        for index in range(2):
            copies.append(
                pltpu.make_async_remote_copy(
                    src_ref=to_core.at[index, :, columns],
                    dst_ref=from_core.at[part, index],
                    send_sem=core_send.at[part, index],
                    recv_sem=core_recv.at[part, index],
                    device_id={"tp": mate},
                    device_id_type=MESH,
                )
            )
        return copies

    core_copies = [core_copy(part) for part in range(2)]
    for part in (1, 0):
        for index in range(2):
            core_copies[part][index].start()

    slots = groups * capacity
    hot_ref[...] = (
        (target == lax.broadcasted_iota(jnp.int32, (slots, rows), 0).astype(jnp.float32))
        .astype(jnp.float32)
        .astype(jnp.bfloat16)
    )
    coded = position + 1
    line = lax.broadcasted_iota(jnp.int32, (16, rows), 0)
    digits = (
        jnp.where(line < 8, coded // 32, lax.rem(coded, 32)).astype(jnp.float32).astype(jnp.bfloat16)
    )

    def place_copy(dest):
        return pltpu.make_async_remote_copy(
            src_ref=place_bins.at[dest],
            dst_ref=place_ref.at[me],
            send_sem=place_send.at[dest],
            recv_sem=place_recv.at[me],
            device_id={"req": dest},
            device_id_type=MESH,
        )

    def bin_places(dest):
        found = lax.dot_general(
            digits,
            hot_ref[pl.ds(pl.multiple_of(dest * capacity, capacity), capacity), :],
            NT,
            preferred_element_type=jnp.float32,
        )
        return (found[:8] * 32.0 + found[8:]).astype(jnp.int32)

    def send_places(step, carry):
        dest = lax.rem(me + step, groups)
        place_bins[dest] = bin_places(dest)
        place_copy(dest).start()
        return carry

    lax.fori_loop(1, groups, send_places, 0)
    place_ref[me] = bin_places(me)

    chip_copies = {}
    for part in (1, 0):
        columns = pl.ds(part * width, width)
        for index in range(2):
            core_copies[part][index].wait()
        other = 1 - half
        to_chip[part] = (
            partial_ref[other * 2 + side, :, columns] + from_core[part, other].astype(jnp.float32)
        ).astype(jnp.bfloat16)
        copy = pltpu.make_async_remote_copy(
            src_ref=to_chip.at[part],
            dst_ref=from_chip.at[part],
            send_sem=chip_send.at[part],
            recv_sem=chip_recv.at[part],
            device_id={"tp": far},
            device_id_type=MESH,
        )
        copy.start()
        chip_copies[part] = copy

    def kv_copy(part, dest):
        return pltpu.make_async_remote_copy(
            src_ref=bins_ref.at[part, dest],
            dst_ref=kv_ref.at[part, pl.ds(pl.multiple_of(me * capacity, capacity), capacity)],
            send_sem=kv_send.at[part, dest],
            recv_sem=kv_recv.at[part, me],
            device_id={"req": dest},
            device_id_type=MESH,
        )

    for part in (1, 0):
        columns = pl.ds(part * width, width)
        if part == 0:
            place_column = jnp.sum(
                jnp.where(row_id == column_id, position.astype(jnp.float32), 0.0), axis=1, keepdims=True
            )
            angle = place_column * freq_ref[...]
            cosine = jnp.cos(angle)
            lane = lax.broadcasted_iota(jnp.int32, (rows, width), 1)
            sine = jnp.where(lane < width // 2, -1.0, 1.0) * jnp.sin(angle)
        chip_copies[part].wait()
        summed = (
            partial_ref[half * 2 + side, :, columns]
            + from_core[part, half].astype(jnp.float32)
            + from_chip[part].astype(jnp.float32)
        )
        if part == 0:
            summed = summed * cosine + pltpu.roll(summed, width // 2, 1) * sine
        image = summed.astype(jnp.bfloat16)

        def bin_rows(dest, image=image):
            return jnp.dot(
                hot_ref[pl.ds(pl.multiple_of(dest * capacity, capacity), capacity), :],
                image,
                preferred_element_type=jnp.float32,
            ).astype(jnp.bfloat16)

        def send_rows(step, carry, part=part, bin_rows=bin_rows):
            dest = lax.rem(me + step, groups)
            bins_ref[part, dest] = bin_rows(dest)
            kv_copy(part, dest).start()
            return carry

        lax.fori_loop(1, groups, send_rows, 0)
        kv_ref[part, pl.ds(pl.multiple_of(me * capacity, capacity), capacity)] = bin_rows(me)

    def finish(step, carry):
        peer = lax.rem(me + step, groups)
        place_copy(peer).wait_send()
        pltpu.make_async_copy(
            place_bins.at[peer], place_ref.at[peer], place_recv.at[peer]
        ).wait()
        for part in range(2):
            kv_copy(part, peer).wait_send()
            pltpu.make_async_copy(
                bins_ref.at[part, peer],
                kv_ref.at[part, pl.ds(pl.multiple_of(peer * capacity, capacity), capacity)],
                kv_recv.at[part, peer],
            ).wait()
        return carry

    lax.fori_loop(1, groups, finish, 0)


def route(partial, row_request, row_position, groups, capacity):
    heads, rows, both = partial.shape
    width = both // 2
    slots = groups * capacity
    exponent = np.arange(width // 2, dtype=np.float32) * np.float32(
        -2.0 * math.log(1000000.0) / width
    )
    freqs = np.exp(exponent.astype(np.float32)).astype(np.float32)
    freqs = jnp.asarray(np.concatenate([freqs, freqs])[None])
    vmem = pl.BlockSpec(memory_space=VMEM)
    return pl.pallas_call(
        functools.partial(route_kernel, groups, capacity),
        out_shape=(
            jax.ShapeDtypeStruct((2, slots, width), jnp.bfloat16),
            jax.ShapeDtypeStruct((groups, 8, capacity), jnp.int32),
        ),
        in_specs=[vmem] * 4,
        out_specs=(vmem, vmem),
        scratch_shapes=[
            VMEM((2, rows, both), jnp.bfloat16),
            VMEM((2, 2, rows, width), jnp.bfloat16),
            VMEM((2, rows, width), jnp.bfloat16),
            VMEM((2, rows, width), jnp.bfloat16),
            VMEM((slots, rows), jnp.bfloat16),
            VMEM((2, groups, capacity, width), jnp.bfloat16),
            VMEM((groups, 8, capacity), jnp.int32),
            pltpu.SemaphoreType.DMA((2, 2)),
            pltpu.SemaphoreType.DMA((2, 2)),
            pltpu.SemaphoreType.DMA((2,)),
            pltpu.SemaphoreType.DMA((2,)),
            pltpu.SemaphoreType.DMA((2, groups)),
            pltpu.SemaphoreType.DMA((2, groups)),
            pltpu.SemaphoreType.DMA((groups,)),
            pltpu.SemaphoreType.DMA((groups,)),
        ],
        compiler_params=pltpu.CompilerParams(
            collective_id=0, has_side_effects=True, vmem_limit_bytes=32 * 1024 * 1024
        ),
        name="route",
    )(partial, row_request[None], row_position[None], freqs)


def attend_kernel(length_ref, query_ref, text_ref, kv_ref, place_ref, out_ref, keys, values):
    prompt, width = keys.shape
    slots = kv_ref.shape[1]

    @pl.when(pl.program_id(0) == 0)
    def _():
        if place_ref.shape[0] > 1:
            places = jnp.concatenate(
                [place_ref[source, 0:1, :] for source in range(place_ref.shape[0])], axis=1
            )
        else:
            places = place_ref[0, 0:1, :]
        places = places - 1
        first = jnp.min(jnp.where(places < 0, prompt, places), axis=1, keepdims=True)
        last = jnp.max(places, axis=1, keepdims=True)
        for start in range(0, prompt, Q_BLOCK):
            block = pl.ds(start, Q_BLOCK)
            index = lax.broadcasted_iota(jnp.int32, (Q_BLOCK, slots), 0) + start
            hot = (index == places).astype(jnp.float32).astype(jnp.bfloat16)
            own = lax.broadcasted_iota(jnp.int32, (Q_BLOCK, width), 0) + start
            image = (own >= first) & (own <= last)
            for part, held in ((0, keys), (1, values)):
                found = jnp.dot(hot, kv_ref[part], preferred_element_type=jnp.float32)
                text = text_ref[block, part * width : (part + 1) * width].astype(jnp.float32)
                held[block, 0:width] = jnp.where(image, found, text).astype(jnp.bfloat16)
        values[:, width:] = jnp.ones((prompt, width), jnp.bfloat16)

    length = length_ref[0]
    factor = width**-0.5 * math.log2(math.e)
    row = lax.broadcasted_iota(jnp.int32, (Q_BLOCK, Q_BLOCK), 0)
    column = lax.broadcasted_iota(jnp.int32, (Q_BLOCK, Q_BLOCK), 1)

    def score(head, start):
        query = query_ref[head, start : start + Q_BLOCK, :]
        blocks = []
        for first in range(0, start + Q_BLOCK, Q_BLOCK):
            block = lax.dot_general(
                query, keys[first : first + Q_BLOCK], NT, preferred_element_type=jnp.float32
            )
            if first == start:
                block = jnp.where(column <= row, block, jnp.float32(-1e30))
            blocks.append(block)
        return blocks

    def weigh(head, start, blocks):
        highest = jnp.max(functools.reduce(jnp.maximum, blocks), axis=1, keepdims=True)
        result = None
        for index, block in enumerate(blocks):
            expo = jnp.exp2((block - highest) * factor).astype(jnp.bfloat16)
            part = jnp.dot(
                expo,
                values[index * Q_BLOCK : (index + 1) * Q_BLOCK],
                preferred_element_type=jnp.float32,
            )
            result = part if result is None else result + part
        own = lax.broadcasted_iota(jnp.int32, (Q_BLOCK, width), 0) + start
        attended = jnp.where(own < length, result[:, :width] / result[:, width:], 0.0)
        out_ref[head, start : start + Q_BLOCK, :] = attended.astype(jnp.bfloat16)

    steps = [
        (head, start) for head in range(query_ref.shape[0]) for start in range(0, prompt, Q_BLOCK)
    ]
    held = score(*steps[0])
    for index, step in enumerate(steps):
        later = score(*steps[index + 1]) if index + 1 < len(steps) else None
        weigh(*step, held)
        held = later


def attend(queries, text, kv, places, lengths):
    heads, prompt, width = queries.shape
    return pl.pallas_call(
        attend_kernel,
        out_shape=jax.ShapeDtypeStruct(queries.shape, jnp.bfloat16),
        grid_spec=pltpu.PrefetchScalarGridSpec(
            num_scalar_prefetch=1,
            grid=(heads // HEAD_BLOCK,),
            in_specs=[
                pl.BlockSpec((HEAD_BLOCK, prompt, width), lambda head, _: (head, 0, 0)),
                pl.BlockSpec(text.shape, lambda head, _: (0, 0)),
                pl.BlockSpec(kv.shape, lambda head, _: (0, 0, 0)),
                pl.BlockSpec(places.shape, lambda head, _: (0, 0, 0)),
            ],
            out_specs=pl.BlockSpec((HEAD_BLOCK, prompt, width), lambda head, _: (head, 0, 0)),
            scratch_shapes=[
                VMEM((prompt, width), jnp.bfloat16),
                VMEM((prompt, 2 * width), jnp.bfloat16),
            ],
        ),
        compiler_params=pltpu.CompilerParams(vmem_limit_bytes=48 * 1024 * 1024),
        name="attend",
    )(lengths, queries, text, kv, places)


def per_device(queries, text_kv, image_rows, row_request, row_position, prompt_lengths, kv_weight):
    groups = lax.axis_size("req")
    capacity = 2 * image_rows.shape[0] // groups
    partial = jnp.einsum(
        "rd,dhc->hrc", image_rows, kv_weight, preferred_element_type=jnp.float32
    )
    kv, places = route(partial, row_request, row_position, groups, capacity)
    if capacity % 128:
        places = jnp.broadcast_to(places[:, 0, :].reshape(1, 1, -1), (1, 8, groups * capacity))
    attended = attend(
        jnp.transpose(queries[0], (1, 0, 2)), text_kv[0, :, 0, :], kv, places, prompt_lengths
    )
    return jnp.transpose(attended, (1, 0, 2))[None]


def solution(mesh):
    in_specs = (
        P("req", None, "tp", None),
        P("req", None, "tp", None),
        P("req", "tp"),
        P("req"),
        P("req"),
        P("req"),
        P("tp", None, None),
    )
    out_specs = P("req", None, "tp", None)
    return jax.shard_map(
        per_device, mesh=mesh, in_specs=in_specs, out_specs=out_specs, check_vma=False
    )
```
